256 devices in a mesh: group: 16 (over x, z_hi), fsdp: 16 (over y, z_lo, core).
Axes of the slice: x: 4, y: 4, z: 8 (z_hi: 4, z_lo: 2; z = z_hi * 2 + z_lo), core: 2. Of those that a mesh axis runs over, the one named last changes fastest.
Arguments:
- params: float32 [16, 768, 5120], P('group', 'fsdp'), may hold values from -6 to 6
- moment_one: float32 [16, 768, 5120], P('group', 'fsdp'), may hold values from -4 to 4
- moment_two: float32 [16, 768, 5120], P('group', 'fsdp'), may hold values from 0.05 to 1
- hidden: bfloat16 [16, 8192, 768], P('group', 'fsdp'), may hold values from -6 to 6
- cotangent: bfloat16 [16, 8192, 5120], P('group', 'fsdp'), may hold values from -0.059814453 to 0.059814453
- token_ids: int32 [16, 8192], P('group', 'fsdp'), may hold values from 0 to 31999, as said below
- step: int32 [1], replicated, may hold values from 0 to 63
Outputs:
- mixed: float32 [16, 768, 5120], P('group', 'fsdp')
- moment_new: float32 [16, 768, 5120], P('group', 'fsdp')
- second_new: float32 [16, 768, 5120], P('group', 'fsdp')
The draws below stay inside these ranges and needn't reach their ends.
Inputs may be any that keep to these rules, and one draw needn't show every extreme that they name: `token_ids`: token slots form padded sequences of 128 slots; each sequence holds ids of 1 or more up to a live length of at least 32 slots, then 0.
All inputs are finite; a program needn't handle non-finite values.
Results may differ from the reference program's by a relative error of at most 0.0003.
Values sent between devices are 32-bit elements; how exact they have to be, the bound alone decides.
A program may use at most 128 MiB of HBM per device.

```python
import math
import jax
import jax.numpy as jnp
from jax import lax

D = 5120
VOCAB = 32000
BUCKET = 768
SEQ = 128
GROUPS = 16
TOKENS = 8192


def draw_token_ids(key, part):
    key_len, key_ids = jax.random.split(key)
    sequences = GROUPS * TOKENS // SEQ
    live_len = jax.random.randint(key_len, (sequences, 1), SEQ // 4, SEQ + 1)
    drawn_ids = jax.random.randint(key_ids, (sequences, SEQ), 1, VOCAB)
    position = jnp.arange(SEQ)[None, :]
    result = jnp.where(position < live_len, drawn_ids, 0)
    return result.reshape(GROUPS, TOKENS).astype(jnp.int32)


def spiked(values, key, source, target, shards_of, factor):
    owner, partner = [(jnp.arange(values.shape[dim]) // (values.shape[dim] // shards_of)).reshape([-1 if axis == dim else 1 for axis in range(values.ndim)]) for dim in (source, target)]
    chosen = jax.random.permutation(key, shards_of)[partner]
    strong = (owner == chosen) | (owner == (partner + shards_of // 2) % shards_of)
    return jnp.where(strong, factor * values, values)


def level_of(key, dims, shards, low, high):
    def one(dim, parts):
        draws = jax.random.uniform(jax.random.fold_in(jax.random.fold_in(key, 6), dim), (parts,), jnp.float32, low / len(shards), high / len(shards))
        return jnp.repeat(jnp.exp(draws), dims[dim] // parts).reshape((-1,) + (1,) * (len(dims) - dim - 1))

    level = one(*shards[0])
    for cut in shards[1:]:
        level = level * one(*cut)
    return level


def scatter_about(own_key, shape, spread, bound, pieces=(), kind=jnp.bfloat16):
    values = jax.random.normal(own_key, shape, jnp.float32) * spread
    if len(pieces) > 0:
        values = level_of(own_key, shape, pieces, -0.22, 0.18) * values
    return jnp.clip(values, min=-bound, max=bound).astype(kind)


def heavy_noise(stream_key, extent, width, bound, pieces, heavy, kind=jnp.bfloat16):
    values = width * jax.random.normal(stream_key, extent, jnp.float32)
    if pieces:
        values = values * level_of(stream_key, extent, pieces, -0.22, 0.18)
    return jnp.clip(spiked(values, jax.random.fold_in(stream_key, 3), *heavy), -bound, bound).astype(kind)


def setup_inputs(seed: int = 0) -> dict:
    key_list = jax.random.split(jax.random.key(seed), 8)
    params = scatter_about(key_list[0], (GROUPS, BUCKET, D), 1.0, 6.0, ((0, 16), (1, 16)), jnp.float32)
    moment_one = scatter_about(key_list[1], (GROUPS, BUCKET, D), 0.5, 4.0, ((0, 16), (1, 16)), jnp.float32)
    moment_two = jnp.clip(jnp.exp(math.log(1.0) - 2.9957323 * jax.random.uniform(key_list[2], (GROUPS, BUCKET, D), jnp.float32) ** level_of(key_list[2], (GROUPS, BUCKET, D), ((0, 16), (1, 16)), -0.2, 0.2)), 0.05, 1.0)
    hidden = heavy_noise(key_list[3], (GROUPS, TOKENS, BUCKET), 1.0, 6.0, ((0, 16), (1, 16)), (1, 2, 16, 2.0))
    cotangent = scatter_about(key_list[4], (GROUPS, TOKENS, D), 0.01, 0.059814453, ((0, 16), (1, 16)))
    token_ids = draw_token_ids(jax.random.fold_in(key_list[7], 71), 0)
    step = jax.random.randint(key_list[6], (1,), 0, 64).astype(jnp.int32)
    return dict(params=params, moment_one=moment_one, moment_two=moment_two, hidden=hidden, cotangent=cotangent, token_ids=token_ids, step=step)


beta_one = 0.9
beta_two = 0.95
learn_rate = 0.02
weight_decay = 0.1
epsilon = 1e-08

def adam_step(param, moment, second, grad, steps_done):
    moment_next = beta_one * moment + (1.0 - beta_one) * grad
    second_next = beta_two * second + (1.0 - beta_two) * grad * grad
    corr_one = 1.0 - jnp.power(beta_one, steps_done)
    corr_two = 1.0 - jnp.power(beta_two, steps_done)
    scaled = moment_next / corr_one / (jnp.sqrt(second_next / corr_two) + epsilon)
    return (param - learn_rate * (scaled + weight_decay * param), moment_next, second_next)

def group_grad(operands):
    hidden_group, masked_group = operands
    return jnp.dot(hidden_group.T, masked_group, preferred_element_type=jnp.float32)

def reference(params, moment_one, moment_two, hidden, cotangent, token_ids, step):
    masked = jnp.where(token_ids[:, :, None] > 0, cotangent, jnp.zeros((), jnp.bfloat16))
    grads = lax.map(group_grad, (hidden, masked))
    steps_done = (step[0] + 1).astype(jnp.float32)
    fresh, moment_new, second_new = adam_step(params, moment_one, moment_two, grads, steps_done)
    distance = jnp.left_shift(jnp.int32(1), (step[0] % 4).astype(jnp.int32))
    source_rows = ((jnp.arange(GROUPS, dtype=jnp.int32) - distance) % GROUPS).astype(jnp.int32)
    mixed = 0.5 * (fresh + fresh[source_rows])
    return (mixed, moment_new, second_new)
```

```python
import functools

import jax
import jax.numpy as jnp
from jax import lax
from jax.experimental import pallas as pl
from jax.experimental.pallas import tpu as pltpu
from jax.sharding import PartitionSpec as P

MESH = pl.DeviceIdType.MESH

beta_one = 0.9
beta_two = 0.95
learn_rate = 0.02
weight_decay = 0.1
epsilon = 1e-08

LANES = 128
RING = 4


def kernel(
    distance,
    groups,
    steps,
    rows,
    corr_ref,
    ids_ref,
    params_hbm,
    one_hbm,
    two_hbm,
    hidden_hbm,
    cot_hbm,
    mixed_ref,
    one_out,
    two_out,
    hid,
    left_t,
    cot,
    par,
    one,
    two,
    snd,
    acc,
    r_core,
    r_far,
    r_left,
    r_right,
    z_snd,
    z_rcv,
    fresh,
    g_rcv,
    load_sem,
    cot_sem,
    core_s,
    core_r,
    y_s,
    y_r,
    z_s,
    z_r,
    g_s,
    g_r,
):
    group = lax.axis_index("group")
    place = lax.axis_index("fsdp")
    y = place // 4
    z = (place // 2) % 2
    core = place % 2
    y_next, y_prev, y_far = (y + 1) % RING, (y + 3) % RING, (y + 2) % RING
    right = (group, y_next * 4 + z * 2 + core)
    left = (group, y_prev * 4 + z * 2 + core)
    twin = (group, y * 4 + z * 2 + (1 - core))
    across = (group, y * 4 + (1 - z) * 2 + core)
    below = ((group + distance) % groups, place)
    above = ((group + groups - distance) % groups, place)

    hidden_load = pltpu.make_async_copy(hidden_hbm.at[0], hid, load_sem.at[0])
    hidden_load.start()

    def cot_load(k):
        columns = pl.ds(pl.multiple_of(k * 2 * LANES, 2 * LANES), 2 * LANES)
        return pltpu.make_async_copy(cot_hbm.at[0, :, columns], cot.at[k], cot_sem.at[k])

    def start_cot(k, carry):
        cot_load(k).start()
        return carry

    lax.fori_loop(0, steps, start_cot, 0)
    state_loads = [
        pltpu.make_async_copy(source.at[0], target, load_sem.at[1 + i])
        for i, (source, target) in enumerate(((params_hbm, par), (one_hbm, one), (two_hbm, two)))
    ]
    for load in state_loads:
        load.start()

    barrier = pltpu.get_barrier_semaphore()
    partners = [right, left, twin, across, below]
    if 2 * distance != groups:
        partners.append(above)
    for partner in partners:
        pl.semaphore_signal(barrier, inc=1, device_id=partner, device_id_type=MESH)

    hidden_load.wait()
    live = ids_ref[...] > 0
    half = 8 * rows
    for h in range(2):
        turned = jnp.transpose(hid[:, h * half : (h + 1) * half].astype(jnp.float32))
        turned = jnp.where(live, turned, 0.0).astype(jnp.bfloat16)
        for j in range(8):
            owner = h * 8 + j
            slot = 1 - core if owner % 2 == 0 else core
            left_t[slot, owner // 2] = turned[j * rows : (j + 1) * rows]

    pl.semaphore_wait(barrier, len(partners))

    def copy(source, target, send, recv, device):
        return pltpu.make_async_remote_copy(
            src_ref=source,
            dst_ref=target,
            send_sem=send,
            recv_sem=recv,
            device_id=device,
            device_id_type=MESH,
        )

    def core_copy(k):
        return copy(snd.at[k], r_core.at[k], core_s.at[k], core_r.at[k], twin)

    def y_copy(k, i):
        source, target, device = (
            (acc.at[k, 0, y_far], r_far.at[k, 0], right),
            (acc.at[k, 1, y_far], r_far.at[k, 1], left),
            (acc.at[k, 0, y_prev], r_right.at[k, 0], left),
            (acc.at[k, 1, y_next], r_left.at[k, 1], right),
            (acc.at[k, 0, y_next], r_left.at[k, 0], right),
            (acc.at[k, 1, y_prev], r_right.at[k, 1], left),
        )[i]
        return copy(source, target, y_s.at[k, i], y_r.at[k, i], device)

    def z_copy(k):
        return copy(z_snd.at[k], z_rcv.at[k], z_s.at[k], z_r.at[k], across)

    def g_copy(k):
        return copy(fresh.at[k], g_rcv.at[k], g_s.at[k], g_r.at[k], below)

    inv_one = corr_ref[0]
    inv_two = corr_ref[1]

    def multiply(k):
        cot_load(k).wait()
        for slot, target in ((0, snd), (1, acc)):
            product = jnp.dot(
                left_t[slot].reshape(8 * rows, left_t.shape[-1]),
                cot[k],
                preferred_element_type=jnp.float32,
            ).reshape(RING, 2, rows, 2 * LANES)
            target[k, 0] = product[..., :LANES]
            target[k, 1] = product[..., LANES:]
            if slot == 0:
                core_copy(k).start()

    def add_core(k):
        core_copy(k).wait_recv()
        acc[k] += r_core[k]
        for i in range(4):
            y_copy(k, i).start()

    def add_far(k):
        y_copy(k, 0).wait_recv()
        acc[k, 0, y_next] += r_far[k, 0]
        y_copy(k, 4).start()
        y_copy(k, 1).wait_recv()
        acc[k, 1, y_prev] += r_far[k, 1]
        y_copy(k, 5).start()

    def add_near(k):
        for i in range(2, 6):
            y_copy(k, i).wait_recv()
        for p in range(2):
            z_snd[k, p] = acc[k, p, y, 1 - z] + r_left[k, p, 1 - z] + r_right[k, p, 1 - z]
        z_copy(k).start()

    def update(k):
        z_copy(k).wait_recv()
        for p in range(2):
            columns = pl.ds(pl.multiple_of((2 * k + p) * LANES, LANES), LANES)
            grad = acc[k, p, y, z] + r_left[k, p, z] + r_right[k, p, z] + z_rcv[k, p]
            one_next = beta_one * one[:, columns] + (1.0 - beta_one) * grad
            two_next = beta_two * two[:, columns] + (1.0 - beta_two) * grad * grad
            one_out[0, :, columns] = one_next
            two_out[0, :, columns] = two_next
            scaled = (one_next * inv_one) / (jnp.sqrt(two_next * inv_two) + epsilon)
            held = par[:, columns]
            fresh[k, p] = held - learn_rate * (scaled + weight_decay * held)
        g_copy(k).start()

    def mix(k):
        g_copy(k).wait_recv()
        for p in range(2):
            columns = pl.ds(pl.multiple_of((2 * k + p) * LANES, LANES), LANES)
            mixed_ref[0, :, columns] = 0.5 * (fresh[k, p] + g_rcv[k, p])
        core_copy(k).wait_send()
        for i in range(6):
            y_copy(k, i).wait_send()
        z_copy(k).wait_send()
        g_copy(k).wait_send()

    stages = ((multiply, 0), (add_core, 1), (add_far, 2), (add_near, 4), (update, 5), (mix, 7))

    for load in state_loads:
        load.wait()

    def body(t, carry):
        for stage, lag in stages:

            @pl.when((t >= lag) & (t < steps + lag))
            def _(stage=stage, lag=lag):
                stage(t - lag)

        return carry

    lax.fori_loop(0, steps + stages[-1][1], body, 0)


def fused(distance, groups, corr, token_ids, params, moment_one, moment_two, hidden, cotangent):
    _, rows, width = params.shape
    _, tokens, bucket = hidden.shape
    steps = width // (2 * LANES)
    f32 = jnp.float32
    whole = pltpu.VMEM((steps, 2, RING, 2, rows, LANES), f32)
    unit = pltpu.VMEM((steps, 2, 2, rows, LANES), f32)
    own = pltpu.VMEM((steps, 2, rows, LANES), f32)
    shard = pltpu.VMEM((rows, width), f32)
    dma = pltpu.SemaphoreType.DMA
    out = jax.ShapeDtypeStruct(params.shape, f32)
    anywhere = pl.BlockSpec(memory_space=pl.ANY)
    vmem = pl.BlockSpec(memory_space=pltpu.VMEM)
    return pl.pallas_call(
        functools.partial(kernel, distance, groups, steps, rows),
        out_shape=(out, out, out),
        in_specs=[pl.BlockSpec(memory_space=pltpu.SMEM), vmem] + [anywhere] * 5,
        out_specs=(vmem, vmem, vmem),
        scratch_shapes=[
            pltpu.VMEM((tokens, bucket), jnp.bfloat16),
            pltpu.VMEM((2, 8, rows, tokens), jnp.bfloat16),
            pltpu.VMEM((steps, tokens, 2 * LANES), jnp.bfloat16),
            shard,
            shard,
            shard,
            whole,
            whole,
            whole,
            unit,
            unit,
            unit,
            own,
            own,
            own,
            own,
            dma((4,)),
            dma((steps,)),
            dma((steps,)),
            dma((steps,)),
            dma((steps, 6)),
            dma((steps, 6)),
            dma((steps,)),
            dma((steps,)),
            dma((steps,)),
            dma((steps,)),
        ],
        compiler_params=pltpu.CompilerParams(
            collective_id=distance.bit_length(),
            has_side_effects=True,
            vmem_limit_bytes=60 * 1024 * 1024,
        ),
        cost_estimate=pl.CostEstimate(
            flops=2 * tokens * bucket * width,
            bytes_accessed=2 * tokens * (bucket + width) + 24 * rows * width,
            transcendentals=rows * width,
        ),
    )(corr, token_ids, params, moment_one, moment_two, hidden, cotangent)


def solution(mesh):
    groups = mesh.shape["group"]

    def per_device(params, moment_one, moment_two, hidden, cotangent, token_ids, step):
        steps_done = (step[0] + 1).astype(jnp.float32)
        corr = jnp.stack(
            [
                1.0 / (1.0 - jnp.power(beta_one, steps_done)),
                1.0 / (1.0 - jnp.power(beta_two, steps_done)),
            ]
        )
        branches = [functools.partial(fused, 2**level, groups) for level in range(4)]
        return lax.switch(
            step[0] % 4,
            branches,
            corr,
            token_ids,
            params,
            moment_one,
            moment_two,
            hidden,
            cotangent,
        )

    rows = P("group", "fsdp", None)
    return jax.shard_map(
        per_device,
        mesh=mesh,
        in_specs=(rows, rows, rows, rows, rows, P("group", "fsdp"), P()),
        out_specs=(rows, rows, rows),
        check_vma=False,
    )
```

```python
import functools

import jax
import jax.numpy as jnp
from jax import lax
from jax.experimental import pallas as pl
from jax.experimental.pallas import tpu as pltpu
from jax.sharding import PartitionSpec as P

MESH = pl.DeviceIdType.MESH

beta_one = 0.9
beta_two = 0.95
learn_rate = 0.02
weight_decay = 0.1
epsilon = 1e-08

LANES = 128
RING = 4
PREFETCH = 8
EARLY = {1: 6, 2: 6, 4: 3, 8: 3}
STEP_BITS = 16

PLANS = {
    1: (0, (0, 3, 6, 9, 11, 15), ()),
    2: (0, (0, 4, 8, 12, 15, 20), ()),
    4: (18, (0, 2, 5, 8, 11, 15), (0, 2, 6, 9, 12, 16)),
    8: (18, (0, 2, 5, 8, 11, 15), (0, 2, 6, 9, 12, 16)),
}


def power(base, exponent):
    result = jnp.float32(1.0)
    for bit in range(STEP_BITS):
        factor = jnp.float32(base ** (2**bit))
        result = result * jnp.where((exponent >> bit) & 1 == 1, factor, jnp.float32(1.0))
    return result


def kernel(
    distance,
    groups,
    chunks,
    rows,
    step_ref,
    ids_ref,
    params_hbm,
    one_hbm,
    two_hbm,
    hidden_hbm,
    cot_hbm,
    mixed_ref,
    one_out,
    two_out,
    hid,
    left_t,
    cot,
    par,
    one,
    two,
    snd,
    acc,
    r_core,
    y_far_in,
    y_b_in,
    y_c_in,
    z_snd,
    z_rcv,
    q_z_in,
    q_far_in,
    q_b_in,
    q_c_in,
    fresh,
    g_rcv,
    load_sem,
    cot_sem,
    core_s,
    core_r,
    y_s,
    y_r,
    z_s,
    z_r,
    g_s,
    g_r,
):
    z_first, y_lags, q_lags = PLANS[distance]
    y_first = chunks - z_first

    group = lax.axis_index("group")
    place = lax.axis_index("fsdp")
    y = place // 4
    z = (place // 2) % 2
    core = place % 2
    far = (y + 2) % RING

    def along(other_y):
        return (group, other_y * 4 + z * 2 + core)

    twin = (group, y * 4 + z * 2 + (1 - core))
    across = (group, y * 4 + (1 - z) * 2 + core)
    below = ((group + distance) % groups, place)
    above = ((group + groups - distance) % groups, place)

    barrier = pltpu.get_barrier_semaphore()
    partners = [along((y + 1) % RING), along((y + 3) % RING), twin, across, below]
    if 2 * distance != groups:
        partners.append(above)
    for partner in partners:
        pl.semaphore_signal(barrier, inc=1, device_id=partner, device_id_type=MESH)

    hidden_load = pltpu.make_async_copy(hidden_hbm.at[0], hid, load_sem.at[0])
    hidden_load.start()

    def cot_load(k):
        columns = pl.ds(pl.multiple_of(k * LANES, LANES), LANES)
        return pltpu.make_async_copy(cot_hbm.at[0, :, columns], cot.at[k], cot_sem.at[k])

    streams = [(0, y_first)] + ([(y_first, z_first)] if z_first else [])
    for base, count in streams:
        for k in range(min(PREFETCH, count)):
            cot_load(base + k).start()
    state_loads = [
        pltpu.make_async_copy(source.at[0], target, load_sem.at[1 + i])
        for i, (source, target) in enumerate(((params_hbm, par), (one_hbm, one), (two_hbm, two)))
    ]

    done = step_ref[0] + 1
    inv_one = 1.0 / (1.0 - jnp.full((1, LANES), power(beta_one, done)))
    inv_two = 1.0 / (1.0 - jnp.full((1, LANES), power(beta_two, done)))

    hidden_load.wait()
    live = ids_ref[...] > 0
    half = 8 * rows
    for h in range(2):
        turned = jnp.transpose(hid[:, h * half : (h + 1) * half].astype(jnp.float32))
        turned = jnp.where(live, turned, 0.0).astype(jnp.bfloat16)
        for j in range(8):
            owner = h * 8 + j
            slot = 1 - core if owner % 2 == 0 else core
            left_t[slot, owner // 2] = turned[j * rows : (j + 1) * rows]

    for load in state_loads:
        load.start()

    def copy(source, target, send, recv, device):
        return pltpu.make_async_remote_copy(
            src_ref=source,
            dst_ref=target,
            send_sem=send,
            recv_sem=recv,
            device_id=device,
            device_id_type=MESH,
        )

    def columns_of(k):
        return pl.ds(pl.multiple_of(k * LANES, LANES), LANES)

    def core_copy(k):
        return copy(snd.at[k], r_core.at[k], core_s.at[k], core_r.at[k], twin)

    def g_copy(k):
        return copy(fresh.at[k], g_rcv.at[k], g_s.at[k], g_r.at[k], below)

    def multiply(k, z_major, send=True):
        cot_load(k).wait()
        for slot, target in ((0, snd), (1, acc)):
            product = jnp.dot(
                left_t[slot].reshape(8 * rows, left_t.shape[-1]),
                cot[k],
                preferred_element_type=jnp.float32,
            )
            for block in range(8):
                there = (block % 2) * RING + block // 2 if z_major else block
                target[k, there] = product[block * rows : (block + 1) * rows]
            if slot == 0 and send:
                core_copy(k).start()

    def prefetch(k, end):
        @pl.when(k + PREFETCH < end)
        def _():
            cot_load(k + PREFETCH).start()

    def adam(k, grad):
        columns = columns_of(k)
        one_next = beta_one * one[:, columns] + (1.0 - beta_one) * grad
        two_next = beta_two * two[:, columns] + (1.0 - beta_two) * grad * grad
        one_out[0, :, columns] = one_next
        two_out[0, :, columns] = two_next
        scaled = (one_next * inv_one) / (jnp.sqrt(two_next * inv_two) + epsilon)
        held = par[:, columns]
        fresh[k] = held - learn_rate * (scaled + weight_decay * held)
        g_copy(k).start()

    def ring_of(parity):
        return (y + 1 + 2 * parity) % RING, (y + 3 + 2 * parity) % RING

    def mixing(k):
        g_copy(k).wait_recv()
        mixed_ref[0, :, columns_of(k)] = 0.5 * (fresh[k] + g_rcv[k])
        core_copy(k).wait_send()
        g_copy(k).wait_send()

    def y_copies(k):
        to_c, to_b = ring_of(k % 2)

        def of(other):
            return acc.at[k, pl.ds(other * 2, 2)]

        return (
            copy(of(far), y_far_in.at[k], y_s.at[k, 0], y_r.at[k, 0], along(to_c)),
            copy(of(to_b), y_b_in.at[k], y_s.at[k, 1], y_r.at[k, 1], along(to_b)),
            copy(of(to_c), y_c_in.at[k], y_s.at[k, 2], y_r.at[k, 2], along(to_c)),
        )

    def z_copy(k):
        return copy(z_snd.at[k], z_rcv.at[k], z_s.at[k], z_r.at[k], across)

    def y_multiply(k, send=True):
        prefetch(k, y_first)
        multiply(k, False, send)

    def y_core(k):
        core_copy(k).wait_recv()
        acc[k] += r_core[k]
        by_far, by_b, _ = y_copies(k)
        by_far.start()
        by_b.start()

    def y_merge(k):
        by_far, _, by_c = y_copies(k)
        to_c, _ = ring_of(k % 2)
        by_far.wait_recv()
        acc[k, pl.ds(to_c * 2, 2)] += y_far_in[k]
        by_c.start()

    def y_near(k):
        _, by_b, by_c = y_copies(k)
        by_b.wait_recv()
        by_c.wait_recv()
        z_snd[k] = acc[k, y * 2 + 1 - z] + y_b_in[k, 1 - z] + y_c_in[k, 1 - z]
        z_copy(k).start()

    def y_update(k):
        z_copy(k).wait_recv()
        adam(k, acc[k, y * 2 + z] + y_b_in[k, z] + y_c_in[k, z] + z_rcv[k])

    def y_mix(k):
        mixing(k)
        for moved in y_copies(k):
            moved.wait_send()
        z_copy(k).wait_send()

    def q_z_copy(k):
        j = k - y_first
        return copy(
            acc.at[k, pl.ds((1 - z) * RING, RING)], q_z_in.at[j], z_s.at[k], z_r.at[k], across
        )

    def q_copies(k):
        j = k - y_first
        to_c, to_b = ring_of((j + 1) % 2)

        def of(other):
            return acc.at[k, z * RING + other]

        return (
            copy(of(far), q_far_in.at[j], y_s.at[k, 0], y_r.at[k, 0], along(to_c)),
            copy(of(to_b), q_b_in.at[j], y_s.at[k, 1], y_r.at[k, 1], along(to_b)),
            copy(of(to_c), q_c_in.at[j], y_s.at[k, 2], y_r.at[k, 2], along(to_c)),
        )

    def q_multiply(k, send=True):
        prefetch(k, chunks)
        multiply(k, True, send)

    def q_core(k):
        core_copy(k).wait_recv()
        acc[k] += r_core[k]
        q_z_copy(k).start()

    def q_across(k):
        q_z_copy(k).wait_recv()
        acc[k, pl.ds(z * RING, RING)] += q_z_in[k - y_first]
        by_far, by_b, _ = q_copies(k)
        by_far.start()
        by_b.start()

    def q_merge(k):
        by_far, _, by_c = q_copies(k)
        to_c, _ = ring_of((k - y_first + 1) % 2)
        by_far.wait_recv()
        acc[k, z * RING + to_c] += q_far_in[k - y_first]
        by_c.start()

    def q_update(k):
        _, by_b, by_c = q_copies(k)
        by_b.wait_recv()
        by_c.wait_recv()
        j = k - y_first
        adam(k, acc[k, z * RING + y] + q_b_in[j] + q_c_in[j])

    def q_mix(k):
        mixing(k)
        for moved in q_copies(k):
            moved.wait_send()
        q_z_copy(k).wait_send()

    work = [(0, y_first, *pair) for pair in zip((y_multiply, y_core, y_merge, y_near, y_update, y_mix), y_lags)]
    if z_first:
        more = [(y_first, z_first, *pair) for pair in zip((q_multiply, q_core, q_across, q_merge, q_update, q_mix), q_lags)]
        work = [entry for both in zip(work, more) for entry in both]

    early = EARLY[distance]

    def ahead(k, carry):
        y_multiply(k, False)
        if z_first:
            q_multiply(y_first + k, False)
        return carry

    lax.fori_loop(0, early, ahead, 0)
    pl.semaphore_wait(barrier, len(partners))

    def first_core(k, carry):
        for base, _ in streams:
            core_copy(base + k).start()
        return carry

    lax.fori_loop(0, early, first_core, 0)

    def body(t, carry):
        @pl.when(t == early)
        def _():
            for load in state_loads:
                load.wait()

        for base, count, stage, lag in work:

            @pl.when((t >= max(lag, early if lag == 0 else 0)) & (t < count + lag))
            def _(base=base, stage=stage, lag=lag):
                stage(base + t - lag)

        return carry

    first = min(lag for _, _, _, lag in work if lag)
    lax.fori_loop(first, max(count + lag for _, count, _, lag in work), body, 0)


def written(one_ref, two_ref, three_ref, one_out, two_out, three_out, sems):
    moves = [
        pltpu.make_async_copy(source, target, sems.at[i])
        for i, (source, target) in enumerate(((one_ref, one_out), (two_ref, two_out), (three_ref, three_out)))
    ]
    for move in moves:
        move.start()
    for move in moves:
        move.wait()


def write_out(*arrays):
    return pl.pallas_call(
        written,
        out_shape=tuple(jax.ShapeDtypeStruct(array.shape, array.dtype) for array in arrays),
        in_specs=[pl.BlockSpec(memory_space=pl.ANY)] * 3,
        out_specs=(pl.BlockSpec(memory_space=pl.ANY),) * 3,
        scratch_shapes=[pltpu.SemaphoreType.DMA((3,))],
        compiler_params=pltpu.CompilerParams(vmem_limit_bytes=1024 * 1024),
    )(*arrays)


def fused(distance, groups, step, token_ids, params, moment_one, moment_two, hidden, cotangent):
    _, rows, width = params.shape
    _, tokens, bucket = hidden.shape
    chunks = width // LANES
    z_first = PLANS[distance][0]
    y_first, z_slots = chunks - z_first, max(z_first, 1)
    f32 = jnp.float32
    dma = pltpu.SemaphoreType.DMA
    whole = pltpu.VMEM((chunks, 8, rows, LANES), f32)
    shard = pltpu.VMEM((rows, width), f32)
    own = pltpu.VMEM((chunks, rows, LANES), f32)
    unit = pltpu.VMEM((y_first, 2, rows, LANES), f32)
    single = pltpu.VMEM((y_first, rows, LANES), f32)
    q_single = pltpu.VMEM((z_slots, rows, LANES), f32)
    out = jax.ShapeDtypeStruct(params.shape, f32)
    anywhere = pl.BlockSpec(memory_space=pl.ANY)
    vmem = pl.BlockSpec(memory_space=pltpu.VMEM)
    return pl.pallas_call(
        functools.partial(kernel, distance, groups, chunks, rows),
        out_shape=(out, out, out),
        in_specs=[pl.BlockSpec(memory_space=pltpu.SMEM), vmem] + [anywhere] * 5,
        out_specs=(vmem, vmem, vmem),
        scratch_shapes=[
            pltpu.VMEM((tokens, bucket), jnp.bfloat16),
            pltpu.VMEM((2, 8, rows, tokens), jnp.bfloat16),
            pltpu.VMEM((chunks, tokens, LANES), jnp.bfloat16),
            shard,
            shard,
            shard,
            whole,
            whole,
            whole,
            unit,
            unit,
            unit,
            single,
            single,
            pltpu.VMEM((z_slots, RING, rows, LANES), f32),
            q_single,
            q_single,
            q_single,
            own,
            own,
            dma((4,)),
            dma((chunks,)),
            dma((chunks,)),
            dma((chunks,)),
            dma((chunks, 3)),
            dma((chunks, 3)),
            dma((chunks,)),
            dma((chunks,)),
            dma((chunks,)),
            dma((chunks,)),
        ],
        compiler_params=pltpu.CompilerParams(
            collective_id=distance.bit_length(),
            has_side_effects=True,
            vmem_limit_bytes=58 * 1024 * 1024,
        ),
        cost_estimate=pl.CostEstimate(
            flops=2 * tokens * bucket * width,
            bytes_accessed=2 * tokens * (bucket + width) + 24 * rows * width,
            transcendentals=rows * width,
        ),
    )(step, token_ids, params, moment_one, moment_two, hidden, cotangent)


def solution(mesh):
    groups = mesh.shape["group"]

    def per_device(params, moment_one, moment_two, hidden, cotangent, token_ids, step):
        branches = [functools.partial(fused, 2**level, groups) for level in range(4)]
        operands = (step, token_ids, params, moment_one, moment_two, hidden, cotangent)
        return write_out(*lax.switch(step[0] & 3, branches, *operands))

    rows = P("group", "fsdp", None)
    return jax.shard_map(
        per_device,
        mesh=mesh,
        in_specs=(rows, rows, rows, rows, rows, P("group", "fsdp"), P()),
        out_specs=(rows, rows, rows),
        check_vma=False,
    )
```

```python
import functools

import jax
import jax.numpy as jnp
from jax import lax
from jax.experimental import pallas as pl
from jax.experimental.pallas import tpu as pltpu
from jax.sharding import PartitionSpec as P

MESH = pl.DeviceIdType.MESH

beta_one = 0.9
beta_two = 0.95
learn_rate = 0.02
weight_decay = 0.1
epsilon = 1e-08

LANES = 128
RING = 4
PREFETCH = 8
EARLY = {1: 6, 2: 6, 4: 3, 8: 3}
STEP_BITS = 16
SPAN = 5

PLANS = {
    1: (0, (0, 3, 6, 9, 11, 15), ()),
    2: (0, (0, 4, 8, 12, 15, 20), ()),
    4: (18, (0, 2, 5, 8, 11, 15), (0, 2, 6, 9, 12, 16)),
    8: (18, (0, 2, 5, 8, 11, 15), (0, 2, 6, 9, 12, 16)),
}


def power(base, exponent):
    result = jnp.float32(1.0)
    for bit in range(STEP_BITS):
        factor = jnp.float32(base ** (2**bit))
        result = result * jnp.where((exponent >> bit) & 1 == 1, factor, jnp.float32(1.0))
    return result


def kernel(
    distance,
    groups,
    chunks,
    rows,
    step_ref,
    ids_ref,
    params_hbm,
    one_hbm,
    two_hbm,
    hidden_hbm,
    cot_hbm,
    mixed_ref,
    one_out,
    two_out,
    hid,
    left_t,
    cot,
    par,
    one,
    two,
    snd,
    acc,
    r_core,
    y_far_in,
    y_near_in,
    z_snd,
    z_rcv,
    q_z_in,
    q_far_in,
    q_near_in,
    fresh,
    g_rcv,
    load_sem,
    cot_sem,
    sent,
    core_r,
    far_r,
    near_r,
    z_r,
    g_r,
):
    z_first, y_lags, q_lags = PLANS[distance]
    y_first = chunks - z_first

    group = lax.axis_index("group")
    place = lax.axis_index("fsdp")
    y = place // 4
    z = (place // 2) % 2
    core = place % 2
    far = (y + 2) % RING

    def along(other_y):
        return (group, other_y * 4 + z * 2 + core)

    twin = (group, y * 4 + z * 2 + (1 - core))
    across = (group, y * 4 + (1 - z) * 2 + core)
    below = ((group + distance) % groups, place)
    above = ((group + groups - distance) % groups, place)

    barrier = pltpu.get_barrier_semaphore()
    partners = [along((y + 1) % RING), along((y + 3) % RING), twin, across, below]
    if 2 * distance != groups:
        partners.append(above)
    for partner in partners:
        pl.semaphore_signal(barrier, inc=1, device_id=partner, device_id_type=MESH)

    hidden_load = pltpu.make_async_copy(hidden_hbm.at[0], hid, load_sem.at[0])
    hidden_load.start()

    def cot_load(k):
        slot = jnp.where(k < y_first, k % PREFETCH, PREFETCH + (k - y_first) % PREFETCH)
        columns = pl.ds(pl.multiple_of(k * LANES, LANES), LANES)
        return pltpu.make_async_copy(cot_hbm.at[0, :, columns], cot.at[k], cot_sem.at[slot])

    streams = [(0, y_first)] + ([(y_first, z_first)] if z_first else [])
    for base, count in streams:
        for k in range(min(PREFETCH, count)):
            cot_load(base + k).start()
    state_loads = [
        pltpu.make_async_copy(source.at[0], target, load_sem.at[1 + i])
        for i, (source, target) in enumerate(((params_hbm, par), (one_hbm, one), (two_hbm, two)))
    ]

    done = step_ref[0] + 1
    inv_one = 1.0 / (1.0 - jnp.full((1, LANES), power(beta_one, done)))
    inv_two = 1.0 / (1.0 - jnp.full((1, LANES), power(beta_two, done)))

    hidden_load.wait()
    live = ids_ref[...] > 0
    half = 8 * rows
    for h in range(2):
        turned = jnp.transpose(hid[:, h * half : (h + 1) * half].astype(jnp.float32))
        turned = jnp.where(live, turned, 0.0).astype(jnp.bfloat16)
        for j in range(8):
            owner = h * 8 + j
            slot = 1 - core if owner % 2 == 0 else core
            left_t[slot, owner // 2] = turned[j * rows : (j + 1) * rows]

    for load in state_loads:
        load.start()

    def copy(k, source, target, recv, device):
        return pltpu.make_async_remote_copy(
            src_ref=source,
            dst_ref=target,
            send_sem=sent.at[k // SPAN],
            recv_sem=recv,
            device_id=device,
            device_id_type=MESH,
        )

    def columns_of(k):
        return pl.ds(pl.multiple_of(k * LANES, LANES), LANES)

    def core_copy(k):
        return copy(k, snd.at[k], r_core.at[k], core_r.at[k], twin)

    def g_copy(k):
        return copy(k, fresh.at[k], g_rcv.at[k], g_r.at[k], below)

    def prefetch(k, end):
        @pl.when(k + PREFETCH < end)
        def _():
            cot_load(k + PREFETCH).start()

    def multiply(k, end, z_major, send):
        cot_load(k).wait()
        prefetch(k, end)
        for slot, target in ((0, snd), (1, acc)):
            product = jnp.dot(
                left_t[slot].reshape(8 * rows, left_t.shape[-1]),
                cot[k],
                preferred_element_type=jnp.float32,
            )
            for block in range(8):
                there = (block % 2) * RING + block // 2 if z_major else block
                target[k, there] = product[block * rows : (block + 1) * rows]
            if slot == 0 and send:
                core_copy(k).start()

    def adam(k, grad):
        columns = columns_of(k)
        one_next = beta_one * one[:, columns] + (1.0 - beta_one) * grad
        two_next = beta_two * two[:, columns] + (1.0 - beta_two) * grad * grad
        one_out[0, :, columns] = one_next
        two_out[0, :, columns] = two_next
        scaled = (one_next * inv_one) / (jnp.sqrt(two_next * inv_two) + epsilon)
        held = par[:, columns]
        fresh[k] = held - learn_rate * (scaled + weight_decay * held)
        g_copy(k).start()

    def ring_of(parity):
        return (y + 1 + 2 * parity) % RING, (y + 3 + 2 * parity) % RING

    def mixing(k):
        g_copy(k).wait_recv()
        mixed_ref[0, :, columns_of(k)] = 0.5 * (fresh[k] + g_rcv[k])

    def y_copies(k):
        to_c, to_b = ring_of(k % 2)

        def of(other):
            return acc.at[k, pl.ds(other * 2, 2)]

        return (
            copy(k, of(far), y_far_in.at[k], far_r.at[k], along(to_c)),
            copy(k, of(to_b), y_near_in.at[k, 0], near_r.at[k], along(to_b)),
            copy(k, of(to_c), y_near_in.at[k, 1], near_r.at[k], along(to_c)),
        )

    def near_arrived(k, both):
        copy(k, both, both, near_r.at[k], twin).wait_recv()

    def z_copy(k):
        return copy(k, z_snd.at[k], z_rcv.at[k], z_r.at[k], across)

    def y_multiply(k, send=True):
        multiply(k, y_first, False, send)

    def y_core(k):
        core_copy(k).wait_recv()
        acc[k] += r_core[k]
        by_far, by_b, _ = y_copies(k)
        by_far.start()
        by_b.start()

    def y_merge(k):
        by_far, _, by_c = y_copies(k)
        to_c, _ = ring_of(k % 2)
        by_far.wait_recv()
        acc[k, pl.ds(to_c * 2, 2)] += y_far_in[k]
        by_c.start()

    def y_near(k):
        near_arrived(k, y_near_in.at[k])
        z_snd[k] = acc[k, y * 2 + 1 - z] + y_near_in[k, 0, 1 - z] + y_near_in[k, 1, 1 - z]
        z_copy(k).start()

    def y_update(k):
        z_copy(k).wait_recv()
        adam(k, acc[k, y * 2 + z] + y_near_in[k, 0, z] + y_near_in[k, 1, z] + z_rcv[k])

    def q_z_copy(k):
        j = k - y_first
        return copy(k, acc.at[k, pl.ds((1 - z) * RING, RING)], q_z_in.at[j], z_r.at[k], across)

    def q_copies(k):
        j = k - y_first
        to_c, to_b = ring_of((j + 1) % 2)

        def of(other):
            return acc.at[k, z * RING + other]

        return (
            copy(k, of(far), q_far_in.at[j], far_r.at[k], along(to_c)),
            copy(k, of(to_b), q_near_in.at[j, 0], near_r.at[k], along(to_b)),
            copy(k, of(to_c), q_near_in.at[j, 1], near_r.at[k], along(to_c)),
        )

    def q_multiply(k, send=True):
        multiply(k, chunks, True, send)

    def q_core(k):
        core_copy(k).wait_recv()
        acc[k] += r_core[k]
        q_z_copy(k).start()

    def q_across(k):
        q_z_copy(k).wait_recv()
        acc[k, pl.ds(z * RING, RING)] += q_z_in[k - y_first]
        by_far, by_b, _ = q_copies(k)
        by_far.start()
        by_b.start()

    def q_merge(k):
        by_far, _, by_c = q_copies(k)
        to_c, _ = ring_of((k - y_first + 1) % 2)
        by_far.wait_recv()
        acc[k, z * RING + to_c] += q_far_in[k - y_first]
        by_c.start()

    def q_update(k):
        j = k - y_first
        near_arrived(k, q_near_in.at[j])
        adam(k, acc[k, z * RING + y] + q_near_in[j, 0] + q_near_in[j, 1])

    work = [(0, y_first, *pair) for pair in zip((y_multiply, y_core, y_merge, y_near, y_update, mixing), y_lags)]
    if z_first:
        more = [(y_first, z_first, *pair) for pair in zip((q_multiply, q_core, q_across, q_merge, q_update, mixing), q_lags)]
        work = [entry for both in zip(work, more) for entry in both]

    early = EARLY[distance]

    def ahead(k, carry):
        y_multiply(k, False)
        if z_first:
            q_multiply(y_first + k, False)
        return carry

    lax.fori_loop(0, early, ahead, 0)
    pl.semaphore_wait(barrier, len(partners))

    def first_core(k, carry):
        for base, _ in streams:
            core_copy(base + k).start()
        return carry

    lax.fori_loop(0, early, first_core, 0)

    def body(t, carry):
        @pl.when(t == early)
        def _():
            for load in state_loads:
                load.wait()

        for base, count, stage, lag in work:

            @pl.when((t >= max(lag, early if lag == 0 else 0)) & (t < count + lag))
            def _(base=base, stage=stage, lag=lag):
                stage(base + t - lag)

        return carry

    first = min(lag for _, _, _, lag in work if lag)
    lax.fori_loop(first, max(count + lag for _, count, _, lag in work), body, 0)

    def left(i, carry):
        size = acc.at[pl.ds(0, 2 * SPAN)]
        copy(i * SPAN, size, size, core_r.at[0], twin).wait_send()
        return carry

    lax.fori_loop(0, chunks // SPAN, left, 0)


def written(one_ref, two_ref, three_ref, one_out, two_out, three_out, sems):
    moves = [
        pltpu.make_async_copy(source, target, sems.at[i])
        for i, (source, target) in enumerate(((one_ref, one_out), (two_ref, two_out), (three_ref, three_out)))
    ]
    for move in moves:
        move.start()
    for move in moves:
        move.wait()


def write_out(*arrays):
    return pl.pallas_call(
        written,
        out_shape=tuple(jax.ShapeDtypeStruct(array.shape, array.dtype) for array in arrays),
        in_specs=[pl.BlockSpec(memory_space=pl.ANY)] * 3,
        out_specs=(pl.BlockSpec(memory_space=pl.ANY),) * 3,
        scratch_shapes=[pltpu.SemaphoreType.DMA((3,))],
        compiler_params=pltpu.CompilerParams(vmem_limit_bytes=1024 * 1024),
    )(*arrays)


def fused(distance, groups, step, token_ids, params, moment_one, moment_two, hidden, cotangent):
    _, rows, width = params.shape
    _, tokens, bucket = hidden.shape
    chunks = width // LANES
    z_first = PLANS[distance][0]
    y_first, z_slots = chunks - z_first, max(z_first, 1)
    f32 = jnp.float32
    dma = pltpu.SemaphoreType.DMA
    whole = pltpu.VMEM((chunks, 8, rows, LANES), f32)
    shard = pltpu.VMEM((rows, width), f32)
    own = pltpu.VMEM((chunks, rows, LANES), f32)
    single = pltpu.VMEM((y_first, rows, LANES), f32)
    out = jax.ShapeDtypeStruct(params.shape, f32)
    anywhere = pl.BlockSpec(memory_space=pl.ANY)
    vmem = pl.BlockSpec(memory_space=pltpu.VMEM)
    return pl.pallas_call(
        functools.partial(kernel, distance, groups, chunks, rows),
        out_shape=(out, out, out),
        in_specs=[pl.BlockSpec(memory_space=pltpu.SMEM), vmem] + [anywhere] * 5,
        out_specs=(vmem, vmem, vmem),
        scratch_shapes=[
            pltpu.VMEM((tokens, bucket), jnp.bfloat16),
            pltpu.VMEM((2, 8, rows, tokens), jnp.bfloat16),
            pltpu.VMEM((chunks, tokens, LANES), jnp.bfloat16),
            shard,
            shard,
            shard,
            whole,
            whole,
            whole,
            pltpu.VMEM((y_first, 2, rows, LANES), f32),
            pltpu.VMEM((y_first, 2, 2, rows, LANES), f32),
            single,
            single,
            pltpu.VMEM((z_slots, RING, rows, LANES), f32),
            pltpu.VMEM((z_slots, rows, LANES), f32),
            pltpu.VMEM((z_slots, 2, rows, LANES), f32),
            own,
            own,
            dma((4,)),
            dma((2 * PREFETCH,)),
            dma((chunks // SPAN,)),
            dma((chunks,)),
            dma((chunks,)),
            dma((chunks,)),
            dma((chunks,)),
            dma((chunks,)),
        ],
        compiler_params=pltpu.CompilerParams(
            collective_id=distance.bit_length(),
            has_side_effects=True,
            vmem_limit_bytes=58 * 1024 * 1024,
        ),
        cost_estimate=pl.CostEstimate(
            flops=2 * tokens * bucket * width,
            bytes_accessed=2 * tokens * (bucket + width) + 24 * rows * width,
            transcendentals=rows * width,
        ),
    )(step, token_ids, params, moment_one, moment_two, hidden, cotangent)


def solution(mesh):
    groups = mesh.shape["group"]

    def per_device(params, moment_one, moment_two, hidden, cotangent, token_ids, step):
        branches = [functools.partial(fused, 2**level, groups) for level in range(4)]
        operands = (step, token_ids, params, moment_one, moment_two, hidden, cotangent)
        return write_out(*lax.switch(step[0] & 3, branches, *operands))

    rows = P("group", "fsdp", None)
    return jax.shard_map(
        per_device,
        mesh=mesh,
        in_specs=(rows, rows, rows, rows, rows, P("group", "fsdp"), P()),
        out_specs=(rows, rows, rows),
        check_vma=False,
    )
```

```python
import functools

import jax
import jax.numpy as jnp
from jax import lax
from jax.experimental import pallas as pl
from jax.experimental.pallas import tpu as pltpu
from jax.sharding import PartitionSpec as P

MESH = pl.DeviceIdType.MESH

beta_one = 0.9
beta_two = 0.95
learn_rate = 0.02
weight_decay = 0.1
epsilon = 1e-08

LANES = 128
RING = 4
PREFETCH = 8
EARLY = {1: 6, 2: 6, 4: 3, 8: 3}
STEP_BITS = 16
REUSE = {1: 16, 2: 16, 4: 12, 8: 12}
SPAN = 5

PLANS = {
    1: (0, (0, 3, 6, 9, 11, 15), ()),
    2: (0, (0, 3, 6, 9, 11, 17), ()),
    4: (18, (0, 3, 5, 8, 11, 15), (0, 4, 7, 9, 12, 16)),
    8: (18, (0, 3, 5, 8, 11, 15), (0, 4, 7, 9, 12, 16)),
}


def power(base, exponent):
    result = jnp.float32(1.0)
    for bit in range(STEP_BITS):
        factor = jnp.float32(base ** (2**bit))
        result = result * jnp.where((exponent >> bit) & 1 == 1, factor, jnp.float32(1.0))
    return result


def kernel(
    distance,
    groups,
    chunks,
    rows,
    step_ref,
    ids_ref,
    params_hbm,
    one_hbm,
    two_hbm,
    hidden_hbm,
    cot_hbm,
    mixed_ref,
    one_out,
    two_out,
    hid,
    left_t,
    cot,
    par,
    one,
    two,
    snd,
    acc,
    r_core,
    y_far_in,
    y_near_in,
    z_snd,
    z_rcv,
    q_z_in,
    q_far_in,
    q_near_in,
    fresh,
    g_rcv,
    load_sem,
    cot_sem,
    sent,
    core_r,
    far_r,
    near_r,
    z_r,
    g_r,
):
    z_first, y_lags, q_lags = PLANS[distance]
    y_first = chunks - z_first

    group = lax.axis_index("group")
    place = lax.axis_index("fsdp")
    y = place // 4
    z = (place // 2) % 2
    core = place % 2
    far = (y + 2) % RING

    def along(other_y):
        return (group, other_y * 4 + z * 2 + core)

    twin = (group, y * 4 + z * 2 + (1 - core))
    across = (group, y * 4 + (1 - z) * 2 + core)
    below = ((group + distance) % groups, place)
    above = ((group + groups - distance) % groups, place)

    barrier = pltpu.get_barrier_semaphore()
    partners = [along((y + 1) % RING), along((y + 3) % RING), twin, across, below]
    if 2 * distance != groups:
        partners.append(above)
    for partner in partners:
        pl.semaphore_signal(barrier, inc=1, device_id=partner, device_id_type=MESH)

    hidden_load = pltpu.make_async_copy(hidden_hbm.at[0], hid, load_sem.at[0])
    hidden_load.start()

    def turn(k, count):
        return jnp.where(k < y_first, k % count, count + (k - y_first) % count)

    def place_of(k):
        return turn(k, REUSE[distance])

    def cot_load(k):
        slot = turn(k, PREFETCH)
        columns = pl.ds(pl.multiple_of(k * LANES, LANES), LANES)
        return pltpu.make_async_copy(cot_hbm.at[0, :, columns], cot.at[k], cot_sem.at[slot])

    streams = [(0, y_first)] + ([(y_first, z_first)] if z_first else [])
    for base, count in streams:
        for k in range(min(PREFETCH, count)):
            cot_load(base + k).start()
    state_loads = [
        pltpu.make_async_copy(source.at[0], target, load_sem.at[1 + i])
        for i, (source, target) in enumerate(((params_hbm, par), (one_hbm, one), (two_hbm, two)))
    ]

    done = step_ref[0] + 1
    inv_one = 1.0 / (1.0 - jnp.full((1, LANES), power(beta_one, done)))
    inv_two = 1.0 / (1.0 - jnp.full((1, LANES), power(beta_two, done)))

    hidden_load.wait()
    live = ids_ref[...] > 0
    half = 8 * rows
    for h in range(2):
        turned = jnp.transpose(hid[:, h * half : (h + 1) * half].astype(jnp.float32))
        turned = jnp.where(live, turned, 0.0).astype(jnp.bfloat16)
        for j in range(8):
            owner = h * 8 + j
            slot = 1 - core if owner % 2 == 0 else core
            left_t[slot, owner // 2] = turned[j * rows : (j + 1) * rows]

    for load in state_loads:
        load.start()

    def copy(k, source, target, recv, device):
        return pltpu.make_async_remote_copy(
            src_ref=source,
            dst_ref=target,
            send_sem=sent.at[k // SPAN],
            recv_sem=recv,
            device_id=device,
            device_id_type=MESH,
        )

    def columns_of(k):
        return pl.ds(pl.multiple_of(k * LANES, LANES), LANES)

    def core_copy(k):
        return copy(k, snd.at[k], r_core.at[k], core_r.at[place_of(k)], twin)

    def g_copy(k):
        return copy(k, fresh.at[k], g_rcv.at[k], g_r.at[k], below)

    def prefetch(k, end):
        @pl.when(k + PREFETCH < end)
        def _():
            cot_load(k + PREFETCH).start()

    def multiply(k, end, z_major, send):
        cot_load(k).wait()
        prefetch(k, end)
        for slot, target in ((0, snd), (1, acc)):
            product = jnp.dot(
                left_t[slot].reshape(8 * rows, left_t.shape[-1]),
                cot[k],
                preferred_element_type=jnp.float32,
            )
            for block in range(8):
                there = (block % 2) * RING + block // 2 if z_major else block
                target[k, there] = product[block * rows : (block + 1) * rows]
            if slot == 0 and send:
                core_copy(k).start()

    def adam(k, grad):
        columns = columns_of(k)
        one_next = beta_one * one[:, columns] + (1.0 - beta_one) * grad
        two_next = beta_two * two[:, columns] + (1.0 - beta_two) * grad * grad
        one_out[0, :, columns] = one_next
        two_out[0, :, columns] = two_next
        scaled = (one_next * inv_one) / (jnp.sqrt(two_next * inv_two) + epsilon)
        held = par[:, columns]
        fresh[k] = held - learn_rate * (scaled + weight_decay * held)
        g_copy(k).start()

    def ring_of(parity):
        return (y + 1 + 2 * parity) % RING, (y + 3 + 2 * parity) % RING

    def mixing(k):
        g_copy(k).wait_recv()
        mixed_ref[0, :, columns_of(k)] = 0.5 * (fresh[k] + g_rcv[k])

    def y_copies(k):
        to_c, to_b = ring_of(k % 2)

        def of(other):
            return acc.at[k, pl.ds(other * 2, 2)]

        return (
            copy(k, of(far), y_far_in.at[k], far_r.at[place_of(k)], along(to_c)),
            copy(k, of(to_b), y_near_in.at[k, 0], near_r.at[place_of(k)], along(to_b)),
            copy(k, of(to_c), y_near_in.at[k, 1], near_r.at[place_of(k)], along(to_c)),
        )

    def near_arrived(k, both):
        copy(k, both, both, near_r.at[place_of(k)], twin).wait_recv()

    def z_copy(k):
        return copy(k, z_snd.at[k], z_rcv.at[k], z_r.at[place_of(k)], across)

    def y_multiply(k, send=True):
        multiply(k, y_first, False, send)

    def y_core(k):
        core_copy(k).wait_recv()
        acc[k] += r_core[k]
        by_far, by_b, _ = y_copies(k)
        by_far.start()
        by_b.start()

    def y_merge(k):
        by_far, _, by_c = y_copies(k)
        to_c, _ = ring_of(k % 2)
        by_far.wait_recv()
        acc[k, pl.ds(to_c * 2, 2)] += y_far_in[k]
        by_c.start()

    def y_near(k):
        near_arrived(k, y_near_in.at[k])
        z_snd[k] = acc[k, y * 2 + 1 - z] + y_near_in[k, 0, 1 - z] + y_near_in[k, 1, 1 - z]
        z_copy(k).start()

    def y_update(k):
        z_copy(k).wait_recv()
        adam(k, acc[k, y * 2 + z] + y_near_in[k, 0, z] + y_near_in[k, 1, z] + z_rcv[k])

    def q_z_copy(k):
        j = k - y_first
        return copy(k, acc.at[k, pl.ds((1 - z) * RING, RING)], q_z_in.at[j], z_r.at[place_of(k)], across)

    def q_copies(k):
        j = k - y_first
        to_c, to_b = ring_of((j + 1) % 2)

        def of(other):
            return acc.at[k, z * RING + other]

        return (
            copy(k, of(far), q_far_in.at[j], far_r.at[place_of(k)], along(to_c)),
            copy(k, of(to_b), q_near_in.at[j, 0], near_r.at[place_of(k)], along(to_b)),
            copy(k, of(to_c), q_near_in.at[j, 1], near_r.at[place_of(k)], along(to_c)),
        )

    def q_multiply(k, send=True):
        multiply(k, chunks, True, send)

    def q_core(k):
        core_copy(k).wait_recv()
        acc[k] += r_core[k]
        q_z_copy(k).start()

    def q_across(k):
        q_z_copy(k).wait_recv()
        acc[k, pl.ds(z * RING, RING)] += q_z_in[k - y_first]
        by_far, by_b, _ = q_copies(k)
        by_far.start()
        by_b.start()

    def q_merge(k):
        by_far, _, by_c = q_copies(k)
        to_c, _ = ring_of((k - y_first + 1) % 2)
        by_far.wait_recv()
        acc[k, z * RING + to_c] += q_far_in[k - y_first]
        by_c.start()

    def q_update(k):
        j = k - y_first
        near_arrived(k, q_near_in.at[j])
        adam(k, acc[k, z * RING + y] + q_near_in[j, 0] + q_near_in[j, 1])

    work = [(0, y_first, *pair) for pair in zip((y_multiply, y_core, y_merge, y_near, y_update, mixing), y_lags)]
    if z_first:
        more = [(y_first, z_first, *pair) for pair in zip((q_multiply, q_core, q_across, q_merge, q_update, mixing), q_lags)]
        work = [entry for both in zip(work, more) for entry in both]

    early = EARLY[distance]

    def ahead(k, carry):
        y_multiply(k, False)
        if z_first:
            q_multiply(y_first + k, False)
        return carry

    lax.fori_loop(0, early, ahead, 0)
    pl.semaphore_wait(barrier, len(partners))

    def first_core(k, carry):
        for base, _ in streams:
            core_copy(base + k).start()
        return carry

    lax.fori_loop(0, early, first_core, 0)

    def body(t, carry):
        @pl.when(t == early)
        def _():
            for load in state_loads:
                load.wait()

        for base, count, stage, lag in work:

            @pl.when((t >= max(lag, early if lag == 0 else 0)) & (t < count + lag))
            def _(base=base, stage=stage, lag=lag):
                stage(base + t - lag)

        return carry

    first = min(lag for _, _, _, lag in work if lag)
    lax.fori_loop(first, max(count + lag for _, count, _, lag in work), body, 0)

    def left(i, carry):
        size = acc.at[pl.ds(0, 2 * SPAN)]
        copy(i * SPAN, size, size, core_r.at[0], twin).wait_send()
        return carry

    lax.fori_loop(0, chunks // SPAN, left, 0)


def written(one_ref, two_ref, three_ref, one_out, two_out, three_out, sems):
    moves = [
        pltpu.make_async_copy(source, target, sems.at[i])
        for i, (source, target) in enumerate(((one_ref, one_out), (two_ref, two_out), (three_ref, three_out)))
    ]
    for move in moves:
        move.start()
    for move in moves:
        move.wait()


def write_out(*arrays):
    return pl.pallas_call(
        written,
        out_shape=tuple(jax.ShapeDtypeStruct(array.shape, array.dtype) for array in arrays),
        in_specs=[pl.BlockSpec(memory_space=pl.ANY)] * 3,
        out_specs=(pl.BlockSpec(memory_space=pl.ANY),) * 3,
        scratch_shapes=[pltpu.SemaphoreType.DMA((3,))],
        compiler_params=pltpu.CompilerParams(vmem_limit_bytes=1024 * 1024),
    )(*arrays)


def fused(distance, groups, step, token_ids, params, moment_one, moment_two, hidden, cotangent):
    _, rows, width = params.shape
    _, tokens, bucket = hidden.shape
    chunks = width // LANES
    z_first = PLANS[distance][0]
    y_first, z_slots = chunks - z_first, max(z_first, 1)
    f32 = jnp.float32
    dma = pltpu.SemaphoreType.DMA
    whole = pltpu.VMEM((chunks, 8, rows, LANES), f32)
    shard = pltpu.VMEM((rows, width), f32)
    own = pltpu.VMEM((chunks, rows, LANES), f32)
    single = pltpu.VMEM((y_first, rows, LANES), f32)
    out = jax.ShapeDtypeStruct(params.shape, f32)
    anywhere = pl.BlockSpec(memory_space=pl.ANY)
    vmem = pl.BlockSpec(memory_space=pltpu.VMEM)
    return pl.pallas_call(
        functools.partial(kernel, distance, groups, chunks, rows),
        out_shape=(out, out, out),
        in_specs=[pl.BlockSpec(memory_space=pltpu.SMEM), vmem] + [anywhere] * 5,
        out_specs=(vmem, vmem, vmem),
        scratch_shapes=[
            pltpu.VMEM((tokens, bucket), jnp.bfloat16),
            pltpu.VMEM((2, 8, rows, tokens), jnp.bfloat16),
            pltpu.VMEM((chunks, tokens, LANES), jnp.bfloat16),
            shard,
            shard,
            shard,
            whole,
            whole,
            whole,
            pltpu.VMEM((y_first, 2, rows, LANES), f32),
            pltpu.VMEM((y_first, 2, 2, rows, LANES), f32),
            single,
            single,
            pltpu.VMEM((z_slots, RING, rows, LANES), f32),
            pltpu.VMEM((z_slots, rows, LANES), f32),
            pltpu.VMEM((z_slots, 2, rows, LANES), f32),
            own,
            own,
            dma((4,)),
            dma(((2 if z_first else 1) * PREFETCH,)),
            dma((chunks // SPAN,)),
            dma(((2 if z_first else 1) * REUSE[distance],)),
            dma(((2 if z_first else 1) * REUSE[distance],)),
            dma(((2 if z_first else 1) * REUSE[distance],)),
            dma(((2 if z_first else 1) * REUSE[distance],)),
            dma((chunks,)),
        ],
        compiler_params=pltpu.CompilerParams(
            collective_id=distance.bit_length(),
            has_side_effects=True,
            vmem_limit_bytes=58 * 1024 * 1024,
        ),
        cost_estimate=pl.CostEstimate(
            flops=2 * tokens * bucket * width,
            bytes_accessed=2 * tokens * (bucket + width) + 24 * rows * width,
            transcendentals=rows * width,
        ),
    )(step, token_ids, params, moment_one, moment_two, hidden, cotangent)


def solution(mesh):
    groups = mesh.shape["group"]

    def per_device(params, moment_one, moment_two, hidden, cotangent, token_ids, step):
        branches = [functools.partial(fused, 2**level, groups) for level in range(4)]
        operands = (step, token_ids, params, moment_one, moment_two, hidden, cotangent)
        return write_out(*lax.switch(step[0] & 3, branches, *operands))

    rows = P("group", "fsdp", None)
    return jax.shard_map(
        per_device,
        mesh=mesh,
        in_specs=(rows, rows, rows, rows, rows, P("group", "fsdp"), P()),
        out_specs=(rows, rows, rows),
        check_vma=False,
    )
```

```python
import functools

import jax
import jax.numpy as jnp
from jax import lax
from jax.experimental import pallas as pl
from jax.experimental.pallas import tpu as pltpu
from jax.sharding import PartitionSpec as P

MESH = pl.DeviceIdType.MESH

beta_one = 0.9
beta_two = 0.95
learn_rate = 0.02
weight_decay = 0.1
epsilon = 1e-08

LANES = 128
RING = 4
PREFETCH = 8
EARLY = {1: 2, 2: 2, 4: 3, 8: 3}
STEP_BITS = 16
REUSE = {1: 16, 2: 16, 4: 12, 8: 12}
SPAN = 5

PLANS = {
    1: (0, (0, 3, 6, 9, 11, 15), ()),
    2: (0, (0, 3, 6, 9, 11, 17), ()),
    4: (18, (0, 3, 5, 8, 11, 15), (0, 4, 7, 9, 12, 16)),
    8: (18, (0, 3, 5, 8, 11, 15), (0, 4, 7, 9, 12, 16)),
}


def power(base, exponent):
    result = jnp.float32(1.0)
    for bit in range(STEP_BITS):
        factor = jnp.float32(base ** (2**bit))
        result = result * jnp.where((exponent >> bit) & 1 == 1, factor, jnp.float32(1.0))
    return result


def kernel(
    distance,
    groups,
    chunks,
    rows,
    step_ref,
    ids_ref,
    params_hbm,
    one_hbm,
    two_hbm,
    hidden_hbm,
    cot_hbm,
    mixed_ref,
    one_out,
    two_out,
    hid,
    left_t,
    cot,
    par,
    one,
    two,
    snd,
    acc,
    r_core,
    y_far_in,
    y_near_in,
    z_snd,
    z_rcv,
    q_z_in,
    q_far_in,
    q_near_in,
    fresh,
    g_rcv,
    load_sem,
    cot_sem,
    sent,
    core_r,
    far_r,
    near_r,
    z_r,
    g_r,
):
    z_first, y_lags, q_lags = PLANS[distance]
    y_first = chunks - z_first

    group = lax.axis_index("group")
    place = lax.axis_index("fsdp")
    y = place // 4
    z = (place // 2) % 2
    core = place % 2
    far = (y + 2) % RING

    def along(other_y):
        return (group, other_y * 4 + z * 2 + core)

    twin = (group, y * 4 + z * 2 + (1 - core))
    across = (group, y * 4 + (1 - z) * 2 + core)
    below = ((group + distance) % groups, place)
    above = ((group + groups - distance) % groups, place)

    barrier = pltpu.get_barrier_semaphore()
    partners = [along((y + 1) % RING), along((y + 3) % RING), twin, across, below]
    if 2 * distance != groups:
        partners.append(above)
    for partner in partners:
        pl.semaphore_signal(barrier, inc=1, device_id=partner, device_id_type=MESH)

    hidden_load = pltpu.make_async_copy(hidden_hbm.at[0], hid, load_sem.at[0])
    hidden_load.start()

    def turn(k, count):
        return jnp.where(k < y_first, k % count, count + (k - y_first) % count)

    def place_of(k):
        return turn(k, REUSE[distance])

    def cot_load(k):
        slot = turn(k, PREFETCH)
        columns = pl.ds(pl.multiple_of(k * LANES, LANES), LANES)
        return pltpu.make_async_copy(cot_hbm.at[0, :, columns], cot.at[k], cot_sem.at[slot])

    streams = [(0, y_first)] + ([(y_first, z_first)] if z_first else [])
    for base, count in streams:
        for k in range(min(PREFETCH, count)):
            cot_load(base + k).start()
    state_loads = [
        pltpu.make_async_copy(source.at[0], target, load_sem.at[1 + i])
        for i, (source, target) in enumerate(((params_hbm, par), (one_hbm, one), (two_hbm, two)))
    ]

    done = step_ref[0] + 1
    inv_one = 1.0 / (1.0 - jnp.full((1, LANES), power(beta_one, done)))
    inv_two = 1.0 / (1.0 - jnp.full((1, LANES), power(beta_two, done)))

    hidden_load.wait()
    live = ids_ref[...] > 0
    half = 8 * rows
    for h in range(2):
        turned = jnp.transpose(hid[:, h * half : (h + 1) * half].astype(jnp.float32))
        turned = jnp.where(live, turned, 0.0).astype(jnp.bfloat16)
        for j in range(8):
            owner = h * 8 + j
            slot = 1 - core if owner % 2 == 0 else core
            left_t[slot, owner // 2] = turned[j * rows : (j + 1) * rows]

    for load in state_loads:
        load.start()

    def copy(k, source, target, recv, device):
        return pltpu.make_async_remote_copy(
            src_ref=source,
            dst_ref=target,
            send_sem=sent.at[k // SPAN],
            recv_sem=recv,
            device_id=device,
            device_id_type=MESH,
        )

    def columns_of(k):
        return pl.ds(pl.multiple_of(k * LANES, LANES), LANES)

    def core_copy(k):
        return copy(k, snd.at[k], r_core.at[k], core_r.at[place_of(k)], twin)

    def g_copy(k):
        return copy(k, fresh.at[k], g_rcv.at[k], g_r.at[k], below)

    def prefetch(k, end):
        @pl.when(k + PREFETCH < end)
        def _():
            cot_load(k + PREFETCH).start()

    def multiply(k, end, z_major, send):
        cot_load(k).wait()
        prefetch(k, end)
        for slot, target in ((0, snd), (1, acc)):
            product = jnp.dot(
                left_t[slot].reshape(8 * rows, left_t.shape[-1]),
                cot[k],
                preferred_element_type=jnp.float32,
            )
            for block in range(8):
                there = (block % 2) * RING + block // 2 if z_major else block
                target[k, there] = product[block * rows : (block + 1) * rows]
            if slot == 0 and send:
                core_copy(k).start()

    def adam(k, grad):
        columns = columns_of(k)
        one_next = beta_one * one[:, columns] + (1.0 - beta_one) * grad
        two_next = beta_two * two[:, columns] + (1.0 - beta_two) * grad * grad
        one_out[0, :, columns] = one_next
        two_out[0, :, columns] = two_next
        scaled = (one_next * inv_one) / (jnp.sqrt(two_next * inv_two) + epsilon)
        held = par[:, columns]
        fresh[k] = held - learn_rate * (scaled + weight_decay * held)
        g_copy(k).start()

    def ring_of(parity):
        return (y + 1 + 2 * parity) % RING, (y + 3 + 2 * parity) % RING

    def mixing(k):
        g_copy(k).wait_recv()
        mixed_ref[0, :, columns_of(k)] = 0.5 * (fresh[k] + g_rcv[k])

    def y_copies(k):
        to_c, to_b = ring_of(k % 2)

        def of(other):
            return acc.at[k, pl.ds(other * 2, 2)]

        return (
            copy(k, of(far), y_far_in.at[k], far_r.at[place_of(k)], along(to_c)),
            copy(k, of(to_b), y_near_in.at[k, 0], near_r.at[place_of(k)], along(to_b)),
            copy(k, of(to_c), y_near_in.at[k, 1], near_r.at[place_of(k)], along(to_c)),
        )

    def near_arrived(k, both):
        copy(k, both, both, near_r.at[place_of(k)], twin).wait_recv()

    def z_copy(k):
        return copy(k, z_snd.at[k], z_rcv.at[k], z_r.at[place_of(k)], across)

    def y_multiply(k, send=True):
        multiply(k, y_first, False, send)

    def y_core(k):
        core_copy(k).wait_recv()
        acc[k] += r_core[k]
        by_far, by_b, _ = y_copies(k)
        by_far.start()
        by_b.start()

    def y_merge(k):
        by_far, _, by_c = y_copies(k)
        to_c, _ = ring_of(k % 2)
        by_far.wait_recv()
        acc[k, pl.ds(to_c * 2, 2)] += y_far_in[k]
        by_c.start()

    def y_near(k):
        near_arrived(k, y_near_in.at[k])
        z_snd[k] = acc[k, y * 2 + 1 - z] + y_near_in[k, 0, 1 - z] + y_near_in[k, 1, 1 - z]
        z_copy(k).start()

    def y_update(k):
        z_copy(k).wait_recv()
        adam(k, acc[k, y * 2 + z] + y_near_in[k, 0, z] + y_near_in[k, 1, z] + z_rcv[k])

    def q_z_copy(k):
        j = k - y_first
        return copy(k, acc.at[k, pl.ds((1 - z) * RING, RING)], q_z_in.at[j], z_r.at[place_of(k)], across)

    def q_copies(k):
        j = k - y_first
        to_c, to_b = ring_of((j + 1) % 2)

        def of(other):
            return acc.at[k, z * RING + other]

        return (
            copy(k, of(far), q_far_in.at[j], far_r.at[place_of(k)], along(to_c)),
            copy(k, of(to_b), q_near_in.at[j, 0], near_r.at[place_of(k)], along(to_b)),
            copy(k, of(to_c), q_near_in.at[j, 1], near_r.at[place_of(k)], along(to_c)),
        )

    def q_multiply(k, send=True):
        multiply(k, chunks, True, send)

    def q_core(k):
        core_copy(k).wait_recv()
        acc[k] += r_core[k]
        q_z_copy(k).start()

    def q_across(k):
        q_z_copy(k).wait_recv()
        acc[k, pl.ds(z * RING, RING)] += q_z_in[k - y_first]
        by_far, by_b, _ = q_copies(k)
        by_far.start()
        by_b.start()

    def q_merge(k):
        by_far, _, by_c = q_copies(k)
        to_c, _ = ring_of((k - y_first + 1) % 2)
        by_far.wait_recv()
        acc[k, z * RING + to_c] += q_far_in[k - y_first]
        by_c.start()

    def q_update(k):
        j = k - y_first
        near_arrived(k, q_near_in.at[j])
        adam(k, acc[k, z * RING + y] + q_near_in[j, 0] + q_near_in[j, 1])

    work = [(0, y_first, *pair) for pair in zip((y_multiply, y_core, y_merge, y_near, y_update, mixing), y_lags)]
    if z_first:
        more = [(y_first, z_first, *pair) for pair in zip((q_multiply, q_core, q_across, q_merge, q_update, mixing), q_lags)]
        work = [entry for both in zip(work, more) for entry in both]

    early = EARLY[distance]

    def ahead(k, carry):
        y_multiply(k, False)
        if z_first:
            q_multiply(y_first + k, False)
        return carry

    lax.fori_loop(0, early, ahead, 0)
    pl.semaphore_wait(barrier, len(partners))

    def first_core(k, carry):
        for base, _ in streams:
            core_copy(base + k).start()
        return carry

    lax.fori_loop(0, early, first_core, 0)

    def body(t, carry):
        @pl.when(t == y_lags[3])
        def _():
            for load in state_loads:
                load.wait()

        for base, count, stage, lag in work:

            @pl.when((t >= max(lag, early if lag == 0 else 0)) & (t < count + lag))
            def _(base=base, stage=stage, lag=lag):
                stage(base + t - lag)

        return carry

    first = min(early, min(lag for _, _, _, lag in work if lag))
    lax.fori_loop(first, max(count + lag for _, count, _, lag in work), body, 0)

    def left(i, carry):
        size = acc.at[pl.ds(0, 2 * SPAN)]
        copy(i * SPAN, size, size, core_r.at[0], twin).wait_send()
        return carry

    lax.fori_loop(0, chunks // SPAN, left, 0)


def written(one_ref, two_ref, three_ref, one_out, two_out, three_out, sems):
    moves = [
        pltpu.make_async_copy(source, target, sems.at[i])
        for i, (source, target) in enumerate(((one_ref, one_out), (two_ref, two_out), (three_ref, three_out)))
    ]
    for move in moves:
        move.start()
    for move in moves:
        move.wait()


def write_out(*arrays):
    return pl.pallas_call(
        written,
        out_shape=tuple(jax.ShapeDtypeStruct(array.shape, array.dtype) for array in arrays),
        in_specs=[pl.BlockSpec(memory_space=pl.ANY)] * 3,
        out_specs=(pl.BlockSpec(memory_space=pl.ANY),) * 3,
        scratch_shapes=[pltpu.SemaphoreType.DMA((3,))],
        compiler_params=pltpu.CompilerParams(vmem_limit_bytes=1024 * 1024),
    )(*arrays)


def fused(distance, groups, step, token_ids, params, moment_one, moment_two, hidden, cotangent):
    _, rows, width = params.shape
    _, tokens, bucket = hidden.shape
    chunks = width // LANES
    z_first = PLANS[distance][0]
    y_first, z_slots = chunks - z_first, max(z_first, 1)
    f32 = jnp.float32
    dma = pltpu.SemaphoreType.DMA
    whole = pltpu.VMEM((chunks, 8, rows, LANES), f32)
    shard = pltpu.VMEM((rows, width), f32)
    own = pltpu.VMEM((chunks, rows, LANES), f32)
    single = pltpu.VMEM((y_first, rows, LANES), f32)
    out = jax.ShapeDtypeStruct(params.shape, f32)
    anywhere = pl.BlockSpec(memory_space=pl.ANY)
    vmem = pl.BlockSpec(memory_space=pltpu.VMEM)
    return pl.pallas_call(
        functools.partial(kernel, distance, groups, chunks, rows),
        out_shape=(out, out, out),
        in_specs=[pl.BlockSpec(memory_space=pltpu.SMEM), vmem] + [anywhere] * 5,
        out_specs=(vmem, vmem, vmem),
        scratch_shapes=[
            pltpu.VMEM((tokens, bucket), jnp.bfloat16),
            pltpu.VMEM((2, 8, rows, tokens), jnp.bfloat16),
            pltpu.VMEM((chunks, tokens, LANES), jnp.bfloat16),
            shard,
            shard,
            shard,
            whole,
            whole,
            whole,
            pltpu.VMEM((y_first, 2, rows, LANES), f32),
            pltpu.VMEM((y_first, 2, 2, rows, LANES), f32),
            single,
            single,
            pltpu.VMEM((z_slots, RING, rows, LANES), f32),
            pltpu.VMEM((z_slots, rows, LANES), f32),
            pltpu.VMEM((z_slots, 2, rows, LANES), f32),
            own,
            own,
            dma((4,)),
            dma(((2 if z_first else 1) * PREFETCH,)),
            dma((chunks // SPAN,)),
            dma(((2 if z_first else 1) * REUSE[distance],)),
            dma(((2 if z_first else 1) * REUSE[distance],)),
            dma(((2 if z_first else 1) * REUSE[distance],)),
            dma(((2 if z_first else 1) * REUSE[distance],)),
            dma((chunks,)),
        ],
        compiler_params=pltpu.CompilerParams(
            collective_id=distance.bit_length(),
            has_side_effects=True,
            vmem_limit_bytes=58 * 1024 * 1024,
        ),
        cost_estimate=pl.CostEstimate(
            flops=2 * tokens * bucket * width,
            bytes_accessed=2 * tokens * (bucket + width) + 24 * rows * width,
            transcendentals=rows * width,
        ),
    )(step, token_ids, params, moment_one, moment_two, hidden, cotangent)


def solution(mesh):
    groups = mesh.shape["group"]

    def per_device(params, moment_one, moment_two, hidden, cotangent, token_ids, step):
        branches = [functools.partial(fused, 2**level, groups) for level in range(4)]
        operands = (step, token_ids, params, moment_one, moment_two, hidden, cotangent)
        return write_out(*lax.switch(step[0] & 3, branches, *operands))

    rows = P("group", "fsdp", None)
    return jax.shard_map(
        per_device,
        mesh=mesh,
        in_specs=(rows, rows, rows, rows, rows, P("group", "fsdp"), P()),
        out_specs=(rows, rows, rows),
        check_vma=False,
    )
```

```python
import functools

import jax
import jax.numpy as jnp
from jax import lax
from jax.experimental import pallas as pl
from jax.experimental.pallas import tpu as pltpu
from jax.sharding import PartitionSpec as P

MESH = pl.DeviceIdType.MESH

beta_one = 0.9
beta_two = 0.95
learn_rate = 0.02
weight_decay = 0.1
epsilon = 1e-08

LANES = 128
RING = 4
PREFETCH = 8
EARLY = {1: 2, 2: 2, 4: 3, 8: 3}
STEP_BITS = 16
REUSE = {1: 16, 2: 16, 4: 12, 8: 12}
SPAN = 5

PLANS = {
    1: (0, (0, 3, 6, 9, 11, 15), ()),
    2: (0, (0, 3, 6, 9, 11, 17), ()),
    4: (18, (0, 3, 5, 8, 11, 15), (0, 4, 7, 9, 12, 16)),
    8: (18, (0, 3, 5, 8, 11, 15), (0, 4, 7, 9, 12, 16)),
}


def power(base, exponent):
    result = jnp.float32(1.0)
    for bit in range(STEP_BITS):
        factor = jnp.float32(base ** (2**bit))
        result = result * jnp.where((exponent >> bit) & 1 == 1, factor, jnp.float32(1.0))
    return result


def kernel(
    distance,
    groups,
    chunks,
    rows,
    step_ref,
    ids_ref,
    params_hbm,
    one_hbm,
    two_hbm,
    hidden_hbm,
    cot_hbm,
    mixed_ref,
    one_out,
    two_out,
    hid,
    left_t,
    cot,
    par,
    one,
    two,
    snd,
    acc,
    r_core,
    y_far_in,
    y_near_in,
    z_snd,
    z_rcv,
    q_z_in,
    q_far_in,
    q_near_in,
    fresh,
    g_rcv,
    load_sem,
    cot_sem,
    sent,
    core_r,
    far_r,
    near_r,
    z_r,
    g_r,
):
    z_first, y_lags, q_lags = PLANS[distance]
    y_first = chunks - z_first

    group = lax.axis_index("group")
    place = lax.axis_index("fsdp")
    y = place // 4
    z = (place // 2) % 2
    core = place % 2
    far = (y + 2) % RING

    def along(other_y):
        return (group, other_y * 4 + z * 2 + core)

    twin = (group, y * 4 + z * 2 + (1 - core))
    across = (group, y * 4 + (1 - z) * 2 + core)
    below = ((group + distance) % groups, place)
    above = ((group + groups - distance) % groups, place)

    hidden_load = pltpu.make_async_copy(hidden_hbm.at[0], hid, load_sem.at[0])
    hidden_load.start()

    barrier = pltpu.get_barrier_semaphore()
    partners = [along((y + 1) % RING), along((y + 3) % RING), twin, across, below]
    if 2 * distance != groups:
        partners.append(above)
    for partner in partners:
        pl.semaphore_signal(barrier, inc=1, device_id=partner, device_id_type=MESH)

    def turn(k, count):
        return jnp.where(k < y_first, k % count, count + (k - y_first) % count)

    def place_of(k):
        return turn(k, REUSE[distance])

    def cot_load(k):
        slot = turn(k, PREFETCH)
        columns = pl.ds(pl.multiple_of(k * LANES, LANES), LANES)
        return pltpu.make_async_copy(cot_hbm.at[0, :, columns], cot.at[k], cot_sem.at[slot])

    streams = [(0, y_first)] + ([(y_first, z_first)] if z_first else [])
    for base, count in streams:
        cot_load(base).start()
    state_loads = [
        pltpu.make_async_copy(source.at[0], target, load_sem.at[1 + i])
        for i, (source, target) in enumerate(((params_hbm, par), (one_hbm, one), (two_hbm, two)))
    ]

    done = step_ref[0] + 1
    inv_one = 1.0 / (1.0 - jnp.full((1, LANES), power(beta_one, done)))
    inv_two = 1.0 / (1.0 - jnp.full((1, LANES), power(beta_two, done)))

    hidden_load.wait()
    for base, count in streams:
        for k in range(1, min(PREFETCH, count)):
            cot_load(base + k).start()
    live = ids_ref[...] > 0
    half = 8 * rows
    for h in range(2):
        turned = jnp.transpose(hid[:, h * half : (h + 1) * half].astype(jnp.float32))
        turned = jnp.where(live, turned, 0.0).astype(jnp.bfloat16)
        for j in range(8):
            owner = h * 8 + j
            slot = 1 - core if owner % 2 == 0 else core
            left_t[slot, owner // 2] = turned[j * rows : (j + 1) * rows]

    for load in state_loads:
        load.start()

    def copy(k, source, target, recv, device):
        return pltpu.make_async_remote_copy(
            src_ref=source,
            dst_ref=target,
            send_sem=sent.at[k // SPAN],
            recv_sem=recv,
            device_id=device,
            device_id_type=MESH,
        )

    def columns_of(k):
        return pl.ds(pl.multiple_of(k * LANES, LANES), LANES)

    def core_copy(k):
        return copy(k, snd.at[k], r_core.at[k], core_r.at[place_of(k)], twin)

    def g_copy(k):
        return copy(k, fresh.at[k], g_rcv.at[k], g_r.at[k], below)

    def prefetch(k, end):
        @pl.when(k + PREFETCH < end)
        def _():
            cot_load(k + PREFETCH).start()

    def multiply(k, end, z_major, send):
        cot_load(k).wait()
        prefetch(k, end)
        for slot, target in ((0, snd), (1, acc)):
            product = jnp.dot(
                left_t[slot].reshape(8 * rows, left_t.shape[-1]),
                cot[k],
                preferred_element_type=jnp.float32,
            )
            for block in range(8):
                there = (block % 2) * RING + block // 2 if z_major else block
                target[k, there] = product[block * rows : (block + 1) * rows]
            if slot == 0 and send:
                core_copy(k).start()

    def adam(k, grad):
        columns = columns_of(k)
        one_next = beta_one * one[:, columns] + (1.0 - beta_one) * grad
        two_next = beta_two * two[:, columns] + (1.0 - beta_two) * grad * grad
        one_out[0, :, columns] = one_next
        two_out[0, :, columns] = two_next
        scaled = (one_next * inv_one) / (jnp.sqrt(two_next * inv_two) + epsilon)
        held = par[:, columns]
        fresh[k] = held - learn_rate * (scaled + weight_decay * held)
        g_copy(k).start()

    def ring_of(parity):
        return (y + 1 + 2 * parity) % RING, (y + 3 + 2 * parity) % RING

    def mixing(k):
        g_copy(k).wait_recv()
        mixed_ref[0, :, columns_of(k)] = 0.5 * (fresh[k] + g_rcv[k])

    def y_copies(k):
        to_c, to_b = ring_of(k % 2)

        def of(other):
            return acc.at[k, pl.ds(other * 2, 2)]

        return (
            copy(k, of(far), y_far_in.at[k], far_r.at[place_of(k)], along(to_c)),
            copy(k, of(to_b), y_near_in.at[k, 0], near_r.at[place_of(k)], along(to_b)),
            copy(k, of(to_c), y_near_in.at[k, 1], near_r.at[place_of(k)], along(to_c)),
        )

    def near_arrived(k, both):
        copy(k, both, both, near_r.at[place_of(k)], twin).wait_recv()

    def z_copy(k):
        return copy(k, z_snd.at[k], z_rcv.at[k], z_r.at[place_of(k)], across)

    def y_multiply(k, send=True):
        multiply(k, y_first, False, send)

    def y_core(k):
        core_copy(k).wait_recv()
        acc[k] += r_core[k]
        by_far, by_b, _ = y_copies(k)
        by_far.start()
        by_b.start()

    def y_merge(k):
        by_far, _, by_c = y_copies(k)
        to_c, _ = ring_of(k % 2)
        by_far.wait_recv()
        acc[k, pl.ds(to_c * 2, 2)] += y_far_in[k]
        by_c.start()

    def y_near(k):
        near_arrived(k, y_near_in.at[k])
        z_snd[k] = acc[k, y * 2 + 1 - z] + y_near_in[k, 0, 1 - z] + y_near_in[k, 1, 1 - z]
        z_copy(k).start()

    def y_update(k):
        z_copy(k).wait_recv()
        adam(k, acc[k, y * 2 + z] + y_near_in[k, 0, z] + y_near_in[k, 1, z] + z_rcv[k])

    def q_z_copy(k):
        j = k - y_first
        return copy(k, acc.at[k, pl.ds((1 - z) * RING, RING)], q_z_in.at[j], z_r.at[place_of(k)], across)

    def q_copies(k):
        j = k - y_first
        to_c, to_b = ring_of((j + 1) % 2)

        def of(other):
            return acc.at[k, z * RING + other]

        return (
            copy(k, of(far), q_far_in.at[j], far_r.at[place_of(k)], along(to_c)),
            copy(k, of(to_b), q_near_in.at[j, 0], near_r.at[place_of(k)], along(to_b)),
            copy(k, of(to_c), q_near_in.at[j, 1], near_r.at[place_of(k)], along(to_c)),
        )

    def q_multiply(k, send=True):
        multiply(k, chunks, True, send)

    def q_core(k):
        core_copy(k).wait_recv()
        acc[k] += r_core[k]
        q_z_copy(k).start()

    def q_across(k):
        q_z_copy(k).wait_recv()
        acc[k, pl.ds(z * RING, RING)] += q_z_in[k - y_first]
        by_far, by_b, _ = q_copies(k)
        by_far.start()
        by_b.start()

    def q_merge(k):
        by_far, _, by_c = q_copies(k)
        to_c, _ = ring_of((k - y_first + 1) % 2)
        by_far.wait_recv()
        acc[k, z * RING + to_c] += q_far_in[k - y_first]
        by_c.start()

    def q_update(k):
        j = k - y_first
        near_arrived(k, q_near_in.at[j])
        adam(k, acc[k, z * RING + y] + q_near_in[j, 0] + q_near_in[j, 1])

    work = [(0, y_first, *pair) for pair in zip((y_multiply, y_core, y_merge, y_near, y_update, mixing), y_lags)]
    if z_first:
        more = [(y_first, z_first, *pair) for pair in zip((q_multiply, q_core, q_across, q_merge, q_update, mixing), q_lags)]
        work = [entry for both in zip(work, more) for entry in both]

    early = EARLY[distance]

    def ahead(k, carry):
        y_multiply(k, False)
        if z_first:
            q_multiply(y_first + k, False)
        return carry

    lax.fori_loop(0, early, ahead, 0)
    pl.semaphore_wait(barrier, len(partners))

    def first_core(k, carry):
        for base, _ in streams:
            core_copy(base + k).start()
        return carry

    lax.fori_loop(0, early, first_core, 0)

    def body(t, carry):
        @pl.when(t == y_lags[3])
        def _():
            for load in state_loads:
                load.wait()

        for base, count, stage, lag in work:

            @pl.when((t >= max(lag, early if lag == 0 else 0)) & (t < count + lag))
            def _(base=base, stage=stage, lag=lag):
                stage(base + t - lag)

        return carry

    first = min(early, min(lag for _, _, _, lag in work if lag))
    lax.fori_loop(first, max(count + lag for _, count, _, lag in work), body, 0)

    def left(i, carry):
        size = acc.at[pl.ds(0, 2 * SPAN)]
        copy(i * SPAN, size, size, core_r.at[0], twin).wait_send()
        return carry

    lax.fori_loop(0, chunks // SPAN, left, 0)


def written(one_ref, two_ref, three_ref, one_out, two_out, three_out, sems):
    moves = [
        pltpu.make_async_copy(source, target, sems.at[i])
        for i, (source, target) in enumerate(((one_ref, one_out), (two_ref, two_out), (three_ref, three_out)))
    ]
    for move in moves:
        move.start()
    for move in moves:
        move.wait()


def write_out(*arrays):
    return pl.pallas_call(
        written,
        out_shape=tuple(jax.ShapeDtypeStruct(array.shape, array.dtype) for array in arrays),
        in_specs=[pl.BlockSpec(memory_space=pl.ANY)] * 3,
        out_specs=(pl.BlockSpec(memory_space=pl.ANY),) * 3,
        scratch_shapes=[pltpu.SemaphoreType.DMA((3,))],
        compiler_params=pltpu.CompilerParams(vmem_limit_bytes=1024 * 1024),
    )(*arrays)


def fused(distance, groups, step, token_ids, params, moment_one, moment_two, hidden, cotangent):
    _, rows, width = params.shape
    _, tokens, bucket = hidden.shape
    chunks = width // LANES
    z_first = PLANS[distance][0]
    y_first, z_slots = chunks - z_first, max(z_first, 1)
    f32 = jnp.float32
    dma = pltpu.SemaphoreType.DMA
    whole = pltpu.VMEM((chunks, 8, rows, LANES), f32)
    shard = pltpu.VMEM((rows, width), f32)
    own = pltpu.VMEM((chunks, rows, LANES), f32)
    single = pltpu.VMEM((y_first, rows, LANES), f32)
    out = jax.ShapeDtypeStruct(params.shape, f32)
    anywhere = pl.BlockSpec(memory_space=pl.ANY)
    vmem = pl.BlockSpec(memory_space=pltpu.VMEM)
    return pl.pallas_call(
        functools.partial(kernel, distance, groups, chunks, rows),
        out_shape=(out, out, out),
        in_specs=[pl.BlockSpec(memory_space=pltpu.SMEM), vmem] + [anywhere] * 5,
        out_specs=(vmem, vmem, vmem),
        scratch_shapes=[
            pltpu.VMEM((tokens, bucket), jnp.bfloat16),
            pltpu.VMEM((2, 8, rows, tokens), jnp.bfloat16),
            pltpu.VMEM((chunks, tokens, LANES), jnp.bfloat16),
            shard,
            shard,
            shard,
            whole,
            whole,
            whole,
            pltpu.VMEM((y_first, 2, rows, LANES), f32),
            pltpu.VMEM((y_first, 2, 2, rows, LANES), f32),
            single,
            single,
            pltpu.VMEM((z_slots, RING, rows, LANES), f32),
            pltpu.VMEM((z_slots, rows, LANES), f32),
            pltpu.VMEM((z_slots, 2, rows, LANES), f32),
            own,
            own,
            dma((4,)),
            dma(((2 if z_first else 1) * PREFETCH,)),
            dma((chunks // SPAN,)),
            dma(((2 if z_first else 1) * REUSE[distance],)),
            dma(((2 if z_first else 1) * REUSE[distance],)),
            dma(((2 if z_first else 1) * REUSE[distance],)),
            dma(((2 if z_first else 1) * REUSE[distance],)),
            dma((chunks,)),
        ],
        compiler_params=pltpu.CompilerParams(
            collective_id=distance.bit_length(),
            has_side_effects=True,
            vmem_limit_bytes=58 * 1024 * 1024,
        ),
        cost_estimate=pl.CostEstimate(
            flops=2 * tokens * bucket * width,
            bytes_accessed=2 * tokens * (bucket + width) + 24 * rows * width,
            transcendentals=rows * width,
        ),
    )(step, token_ids, params, moment_one, moment_two, hidden, cotangent)


def solution(mesh):
    groups = mesh.shape["group"]

    def per_device(params, moment_one, moment_two, hidden, cotangent, token_ids, step):
        branches = [functools.partial(fused, 2**level, groups) for level in range(4)]
        operands = (step, token_ids, params, moment_one, moment_two, hidden, cotangent)
        return write_out(*lax.switch(step[0] & 3, branches, *operands))

    rows = P("group", "fsdp", None)
    return jax.shard_map(
        per_device,
        mesh=mesh,
        in_specs=(rows, rows, rows, rows, rows, P("group", "fsdp"), P()),
        out_specs=(rows, rows, rows),
        check_vma=False,
    )
```
